32 devices in a mesh: groups: 2 (over x), cells: 16 (over z, y, core).
Axes of the slice: x: 2, y: 2, z: 4, core: 2. Of those that a mesh axis runs over, the one named last changes fastest.
Arguments:
- points: float32 [3, 2097152], P(None, ('groups', 'cells')), parts along dimension 1, may hold values from -6 to 2049, as said below
- centroids: float32 [3, 524288], P(None, ('groups', 'cells')), parts along dimension 1, may hold values from -6 to 2049, as said below
- pair_blocks: int32 [16384, 6], P(('groups', 'cells')), parts along dimension 0, may hold values from 0 to 2047, as said below
- pair_count: int32 [16384], P(('groups', 'cells')), parts along dimension 0, may hold values from 1 to 6, as said below
- centroid_nbrs: int32 [4096, 3], P(('groups', 'cells')), parts along dimension 0, may hold values from 0 to 2047, as said below
- sigma2: float32 [2], P('groups'), parts along dimension 0, may hold values from 2 to 4
Outputs:
- displacement: float32 [3, 524288], P(None, ('groups', 'cells')), parts along dimension 1
- sigma2_new: float32 [2], P('groups'), parts along dimension 0
The draws below stay inside these ranges and needn't reach their ends.
There are 2 independent parts, one for each index of `groups`. The reference program is written for one: setup_inputs(seed, part) draws one part's arguments, and reference() takes and returns one part's arrays. A program takes and returns all parts, laid end to end along the dimension named above; each array names one. Nothing has to cross between parts.
Inputs may be any that keep to these rules, and one draw needn't show every extreme that they name: `points`: point coordinates: along track between the point block's home block b // 4 and the next, across track in [0, 1), heights of either sign. `centroids`: centroid coordinates: along track between the block's index and the next, across track in [0, 1), heights of either sign. `pair_blocks`: A row lists 6 distinct blocks out of the 7 consecutive blocks starting at min(max(h - 3, 0), 2041), h = b // 4 the home block of point block b. Only the first pair_count entries of a row of pair_blocks are used. `centroid_nbrs`: A row starts with the block itself, then lists distinct other blocks out of the 7 consecutive blocks starting at min(max(c - 3, 0), 2041), c the row's block.
All inputs are finite; a program needn't handle non-finite values.
Results may differ from the reference program's by a relative error of at most 0.0003.
Values sent between devices are 32-bit elements; how exact they have to be, the bound alone decides.
A program may use at most 128 MiB of HBM per device.

```python
import math
import jax
import jax.numpy as jnp
from jax import lax

PBLK = 512
CBLK = 128
KSLOT = 6
KNBR = 3
REACH = 3
SMOOTH = 4
NPB = 8192
NCB = 2048
NC = 262144


def height_scale(along):
    return 0.5 + 1.5 * along / NCB


def draw_height(key, along, count):
    raw = jnp.clip(jax.random.normal(key, (count,)), -3.0, 3.0)
    return height_scale(along) * raw


def draw_centroids(key, part):
    key_a, key_b, key_c = jax.random.split(key, 3)
    count = NCB * 128
    home = (jnp.arange(count) // 128).astype(jnp.float32)
    along = home + jax.random.uniform(key_a, (count,))
    across = jax.random.uniform(key_b, (count,))
    return jnp.stack([along, across, draw_height(key_c, along, count)]).astype(jnp.float32)


def draw_points(key, part):
    key_a, key_b, key_c = jax.random.split(key, 3)
    count = NPB * 128
    home = (jnp.arange(count) // 128 // (PBLK // CBLK)).astype(jnp.float32)
    along = home + jax.random.uniform(key_a, (count,))
    across = jax.random.uniform(key_b, (count,))
    return jnp.stack([along, across, draw_height(key_c, along, count)]).astype(jnp.float32)


def window_start(home):
    return jnp.clip(home - REACH, 0, NCB - 1 - 2 * REACH)


def draw_pair_blocks(key, part):
    span = 2 * REACH + 1
    home = jnp.arange(NPB) // (PBLK // CBLK)
    scores = jax.random.randint(key, (NPB, span), 0, 1 << 20) * span + jnp.arange(span)[None, :]
    order = jnp.argsort(scores, axis=1)[:, :KSLOT]
    return (window_start(home)[:, None] + order).astype(jnp.int32)


def draw_pair_count(key, part):
    key_a, key_b, key_c, key_d = jax.random.split(key, 4)
    devices = NPB // PBLK
    heavy = jax.random.randint(key_a, (devices,), 0, 3) == 0
    chosen = jax.random.randint(key_b, (), 0, devices)
    heavy = jnp.logical_or(heavy, jnp.arange(devices) == chosen)
    low = jnp.where(heavy, 3, 1)
    high = jnp.where(heavy, KSLOT, 2)
    raw = jax.random.randint(key_c, (devices, PBLK), 0, 1 << 16)
    counts = low[:, None] + raw % (high - low + 1)[:, None]
    spot = jax.random.randint(key_d, (), 0, PBLK)
    counts = counts.at[chosen, spot].set(KSLOT)
    return counts.reshape(NPB).astype(jnp.int32)


def draw_centroid_nbrs(key, part):
    span = 2 * REACH + 1
    own_block = jnp.arange(NCB)
    first = window_start(own_block)
    offsets = jnp.arange(span)
    scores = jax.random.randint(key, (NCB, span), 0, 1 << 20) * span + offsets[None, :]
    scores = jnp.where(first[:, None] + offsets[None, :] == own_block[:, None], -1, scores)
    order = jnp.argsort(scores, axis=1)[:, :KNBR]
    return (first[:, None] + order).astype(jnp.int32)


def setup_inputs(seed: int = 0, part: int = 0) -> dict:
    streams_of = jax.random.split(jax.random.key(seed), 7)
    own_keys = jax.random.split(jax.random.fold_in(streams_of[6], part), 7)
    points = draw_points(jax.random.fold_in(jax.random.fold_in(streams_of[6], part), 71), part)
    centroids = draw_centroids(jax.random.fold_in(jax.random.fold_in(streams_of[6], part), 71), part)
    pair_blocks = draw_pair_blocks(jax.random.fold_in(jax.random.fold_in(streams_of[6], part), 71), part)
    pair_count = draw_pair_count(jax.random.fold_in(jax.random.fold_in(streams_of[6], part), 71), part)
    centroid_nbrs = draw_centroid_nbrs(jax.random.fold_in(jax.random.fold_in(streams_of[6], part), 71), part)
    sigma2 = jnp.clip(jnp.exp(jax.random.uniform(own_keys[5], (1,), jnp.float32, math.log(2.0), math.log(4.0))), 2.0, 4.0)
    return dict(points=points, centroids=centroids, pair_blocks=pair_blocks, pair_count=pair_count, centroid_nbrs=centroid_nbrs, sigma2=sigma2)


OUTLIER = 0.2
SHRINK = 1.0
KERNEL_VAR = 0.5


def reference(points, centroids, pair_blocks, pair_count, centroid_nbrs, sigma2):
    var_old = sigma2[0]
    outlier = (2.0 * math.pi * var_old) ** 1.5 * (OUTLIER / (1.0 - OUTLIER)) * (CBLK / PBLK)
    cen_blocks = centroids.reshape(3, NCB, 128).transpose(1, 0, 2)
    pnt_blocks = points.reshape(3, NPB, 128).transpose(1, 0, 2)
    group_size = math.gcd(64, NPB)
    slot_ids = jnp.arange(KSLOT, dtype=jnp.int32)

    def group_step(state_in, inputs):
        sums_buf, spread, count = state_in
        point_tile, slot_lists, counts = inputs
        cen_tile = jnp.take(cen_blocks, slot_lists, axis=0)
        differences = [point_tile[:, None, component, None, :] - cen_tile[:, :, component, :, None] for component in range(3)]
        distance2 = differences[0] * differences[0] + differences[1] * differences[1] + differences[2] * differences[2]
        alive_mask = (slot_ids[None, :] < counts[:, None]).astype(jnp.float32)
        affinity = jnp.exp(-distance2 / (2.0 * var_old)) * alive_mask[:, :, None, None]
        summed = jnp.sum(affinity, axis=(1, 2))
        normaliser = summed + outlier
        resp = affinity / normaliser[:, None, None, :]
        block_terms = jnp.stack([jnp.sum(resp, axis=3)] + [jnp.sum(resp * part_diff, axis=3) for part_diff in differences], axis=2)
        sums_buf = sums_buf.at[slot_lists.reshape(-1)].add(block_terms.reshape(-1, 4, 128))
        spread = spread + jnp.sum(resp * distance2)
        count = count + jnp.sum(summed / normaliser)
        return (sums_buf, spread, count), None

    init = (jnp.zeros((NCB, 4, 128), jnp.float32), jnp.zeros((), jnp.float32), jnp.zeros((), jnp.float32))
    inputs = (pnt_blocks.reshape(NPB // group_size, group_size, 3, 128),
              pair_blocks.reshape(NPB // group_size, group_size, KSLOT),
              pair_count.reshape(NPB // group_size, group_size))
    (sums_buf, spread, count), _ = lax.scan(group_step, init, inputs)
    mass = sums_buf[:, 0]
    pull = sums_buf[:, 1:4]
    motion = pull / (mass[:, None, :] + SHRINK)

    sgroup = math.gcd(16, NCB)

    def smooth(motion):
        def group_smooth(gidx):
            own_tile = lax.dynamic_slice_in_dim(cen_blocks, gidx * sgroup, sgroup, 0)
            nbr_local = lax.dynamic_slice_in_dim(centroid_nbrs, gidx * sgroup, sgroup, 0)
            nbr_tile = jnp.take(cen_blocks, nbr_local, axis=0)
            nbr_motion = jnp.take(motion, nbr_local, axis=0)
            pieces = [own_tile[:, None, component, :, None] - nbr_tile[:, :, component, None, :] for component in range(3)]
            distance2 = pieces[0] * pieces[0] + pieces[1] * pieces[1] + pieces[2] * pieces[2]
            kernel = jnp.exp(-distance2 / (2.0 * KERNEL_VAR))
            kernel_sum = jnp.sum(kernel, axis=(1, 3))
            weighted = jnp.einsum("sjab,sjkb->ska", kernel, nbr_motion, precision=lax.Precision.HIGHEST)
            return weighted / kernel_sum[:, None, :]
        smoothed = lax.map(group_smooth, jnp.arange(NCB // sgroup))
        return smoothed.reshape(NCB, 3, 128)

    for step in range(SMOOTH):
        motion = smooth(motion)
    cross = jnp.sum(pull * motion)
    energy = jnp.sum(mass[:, None, :] * motion * motion)
    sigma_new = (spread - 2.0 * cross + energy) / (3.0 * count)
    displacement = motion.transpose(1, 0, 2).reshape(3, NC)
    return displacement, jnp.reshape(sigma_new, (1,))
```

```python
import functools
import math

import jax
import jax.numpy as jnp
from jax import lax
from jax.experimental import pallas as pl
from jax.experimental.pallas import tpu as pltpu
from jax.sharding import PartitionSpec as P

REACH = 3
SMOOTH = 4
OUTLIER = 0.2
SHRINK = 1.0
KERNEL_VAR = 0.5
LOG2E = 1.4426950408889634

F32, BF16 = jnp.float32, jnp.bfloat16
KF = 32
H = 16
WIN = 24
DUMMY = WIN - 1
UNROLL = 4
HALO = 24
FRONT = 16


def split3(v):
    high = v.astype(BF16).astype(F32)
    rest = v - high
    mid = rest.astype(BF16).astype(F32)
    return high, mid, rest - mid


def lane_features(ref_a, ref_z, x, y, z, scale, root):
    rows = x.shape[0]
    ones = jnp.ones_like(x)
    x1, x2, x3 = split3(x)
    y1, y2, y3 = split3(y)
    own = split3(-scale * (x * x + y * y))
    height = split3(-root * z)
    half_a = [x1, x2, x1, x2, x3, x1, y1, y2, y1, y2, y3, y1, ones, ones, ones, *own]
    for k, v in enumerate(half_a):
        ref_a[pl.ds(k, rows, stride=KF), :] = v
    for k, v in enumerate([*height, ones, ones, ones]):
        ref_z[pl.ds(15 + k, rows, stride=KF), :] = v


def row_features(ref_t, x, y, z, scale, root, dead=None):
    rows = x.shape[0]
    ones = jnp.ones_like(x)
    x1, x2, x3 = split3(2.0 * scale * x)
    y1, y2, y3 = split3(2.0 * scale * y)
    own = -scale * (x * x + y * y)
    if dead is not None:
        own = jnp.where(dead, -1e9, own)
    feats = [x1, x1, x2, x2, x1, x3, y1, y1, y2, y2, y1, y3, *split3(own), ones, ones, ones]
    for k, v in enumerate(feats + list(split3(root * z))):
        ref_t[pl.ds(k, rows, stride=KF), :] = v


def transpose_features(ref_t, table):
    def step(i, carry):
        for u in range(4):
            j = i * 4 + u
            block = ref_t[pl.ds(pl.multiple_of(j * KF, KF), KF), :]
            table[j] = block.T.astype(BF16)
        return carry

    lax.fori_loop(0, WIN // 4, step, 0)


def pair_weights(table, ref_a, ref_z, l, b):
    at = pl.ds(pl.multiple_of(b * KF, KF), KF)
    right = jnp.concatenate([ref_a[at, :].astype(BF16), ref_z[at, :].astype(BF16)], axis=1)
    d = jnp.dot(table[l], right, preferred_element_type=F32)
    dz = d[:, 128:]
    return jnp.exp2(d[:, :128] - dz * dz)


def pair_kernel(
    nslot, per_home, nchunk, lists, counts, totals, first, sigma2, pts, cen,
    sums, stats, ref_a, ref_z, ref_t, table, wbuf, wacc, rbuf, acc, bsel, lsel,
):
    ch = H * per_home
    var = sigma2[0]
    scale_v = LOG2E / (2.0 * jnp.full((1, 128), var, F32))
    root_v = jnp.sqrt(scale_v)
    base_v = 2.0 * math.pi * jnp.full((1, 128), var, F32)
    outlier = base_v * jnp.sqrt(base_v) * (OUTLIER / (1.0 - OUTLIER) / per_home)
    for ref in (ref_a, ref_z, ref_t, rbuf):
        ref[...] = jnp.zeros_like(ref)
    sums[...] = jnp.zeros_like(sums)

    def chunk(ck, carry):
        spread, count = carry
        prow = pl.ds(pl.multiple_of(ck * ch, ch), ch)
        crow = pl.ds(pl.multiple_of(ck * H, H), WIN)
        origin = (first[0] + ck * H + H // 2).astype(F32)
        px, py = pts[0, prow, :] - origin, pts[1, prow, :]
        cx, cy = cen[0, crow, :] - origin, cen[1, crow, :]
        z0 = pts[2, pl.ds(pl.multiple_of(ck * ch, ch), 8), :][0:1, 0:1]
        pz = pts[2, prow, :] - z0
        cz = cen[2, crow, :] - z0
        lane_features(ref_a, ref_z, px, py, pz, scale_v, root_v)
        dead = lax.broadcasted_iota(jnp.int32, (WIN, 128), 0) == DUMMY
        row_features(ref_t, cx, cy, cz, scale_v, root_v, dead)
        transpose_features(ref_t, table)
        wacc[...] = jnp.zeros_like(wacc)
        acc[...] = jnp.zeros_like(acc)
        total = totals[ck]
        steps = (total + UNROLL - 1) // UNROLL

        def first_pass(i, state):
            b, s = state
            for u in range(UNROLL):
                k = i * UNROLL + u
                bb = jnp.minimum(b, ch - 1)
                at = ck * ch + bb
                l = lists[at * nslot + s] - ck * H
                l = jnp.where(k < total, l, DUMMY)
                bsel[k] = bb
                lsel[k] = l
                w = pair_weights(table, ref_a, ref_z, l, bb)
                wbuf[k] = w.astype(BF16)
                wrow = pl.ds(pl.multiple_of(bb * 8, 8), 8)
                wacc[wrow, :] += jnp.sum(w.reshape(16, 8, 128), axis=0)
                more = s + 1 < counts[at]
                b = jnp.where(more, b, b + 1)
                s = jnp.where(more, s + 1, 0)
            return b, s

        lax.fori_loop(0, steps, first_pass, (jnp.int32(0), jnp.int32(0)))
        weight = wacc[pl.ds(0, ch, stride=8), :]
        for i in range(1, 8):
            weight = weight + wacc[pl.ds(i, ch, stride=8), :]
        inv = 1.0 / (weight + outlier)
        count = count + weight * inv
        square = px * px + py * py + pz * pz
        feats = [inv, inv * px, inv * py, inv * pz, inv * square]
        for k, v in enumerate(feats):
            for t, piece in enumerate(split3(v)):
                rbuf[pl.ds(3 * k + t, ch, stride=16), :] = piece

        def second_pass(i, carry):
            for u in range(UNROLL):
                k = i * UNROLL + u
                b, l = bsel[k], lsel[k]
                r = rbuf[pl.ds(pl.multiple_of(b * 16, 16), 16), :].astype(BF16)
                o = lax.dot_general(
                    r, wbuf[k], (((1,), (1,)), ((), ())), preferred_element_type=F32
                )
                arow = pl.ds(pl.multiple_of(l * 16, 16), 16)
                acc[arow, :] += o
            return carry

        lax.fori_loop(0, steps, second_pass, 0)
        got = []
        for k in range(5):
            v = acc[pl.ds(3 * k, WIN, stride=16), :]
            v = v + acc[pl.ds(3 * k + 1, WIN, stride=16), :]
            got.append(v + acc[pl.ds(3 * k + 2, WIN, stride=16), :])
        mass, sx, sy, sz, sq = got
        pull_x, pull_y, pull_z = sx - cx * mass, sy - cy * mass, sz - cz * mass
        term = sq - (cx * sx + cy * sy + cz * sz) - (cx * pull_x + cy * pull_y + cz * pull_z)
        spread = spread + jnp.where(dead, 0.0, term)
        for k, v in enumerate([mass, pull_x, pull_y, pull_z]):
            sums[k, crow, :] += jnp.where(dead, 0.0, v)
        return spread, count

    init = (jnp.zeros((WIN, 128), F32), jnp.zeros((ch, 128), F32))
    spread, count = lax.fori_loop(0, nchunk, chunk, init)
    stats[0:1, :] = jnp.sum(spread, axis=0, keepdims=True)
    stats[1:2, :] = jnp.sum(count, axis=0, keepdims=True)


def smooth_kernel(
    nblk, nnbr, nbrs, first, sums, own, win, out, stats,
    ref_a, ref_z, ref_t, table, kern, mrow, obuf,
):
    rows = own.shape[1]
    scale = LOG2E / (2.0 * KERNEL_VAR)
    root = math.sqrt(scale)
    for ref in (ref_a, ref_z, ref_t, mrow):
        ref[...] = jnp.zeros_like(ref)
    mrow[pl.ds(9, rows, stride=16), :] = jnp.ones((rows, 128), F32)

    def chunk(ck, carry):
        orow = pl.ds(pl.multiple_of(ck * H, H), H)
        wrow = pl.ds(pl.multiple_of(ck * H, H), WIN)
        origin = (first[0] + ck * H + H // 2).astype(F32)
        z0 = own[2, pl.ds(pl.multiple_of(ck * H, H), 8), :][0:1, 0:1]
        lane_features(
            ref_a, ref_z, own[0, orow, :] - origin, own[1, orow, :], own[2, orow, :] - z0,
            scale, root,
        )
        row_features(
            ref_t, win[0, wrow, :] - origin, win[1, wrow, :], win[2, wrow, :] - z0, scale, root
        )
        transpose_features(ref_t, table)

        def step(i, carry):
            for j in range(2):
                b = i * 2 + j
                at = ck * H + b
                for s in range(nnbr):
                    l = nbrs[at * nnbr + s] - (ck * H - REACH)
                    l = jnp.clip(l, 0, WIN - 1)
                    w = pair_weights(table, ref_a, ref_z, l, b)
                    kern[at, s * 128 : (s + 1) * 128, :] = w.astype(BF16)
            return carry

        lax.fori_loop(0, H // 2, step, 0)
        return carry

    lax.fori_loop(0, rows // H, chunk, 0)

    def store_motion(motion):
        for k, v in enumerate(motion):
            for t, piece in enumerate(split3(v)):
                mrow[pl.ds(3 * k + t, rows, stride=16), :] = piece

    store_motion([sums[1 + c] / (sums[0] + SHRINK) for c in range(3)])
    for r in range(1, SMOOTH + 1):
        lo = FRONT - REACH * (SMOOTH - r)
        n = nblk + 2 * REACH * (SMOOTH - r)

        def step(i, carry):
            for u in range(2):
                at = lo + i * 2 + u
                left = []
                for s in range(nnbr):
                    j = jnp.clip(nbrs[at * nnbr + s], 0, rows - 1)
                    left.append(mrow[pl.ds(pl.multiple_of(j * 16, 16), 16), :].astype(BF16))
                o = jnp.dot(
                    jnp.concatenate(left, axis=1), kern[at], preferred_element_type=F32
                )
                obuf[pl.ds(pl.multiple_of(at * 16, 16), 16), :] = o
            return carry

        if r == 1:
            obuf[...] = jnp.ones_like(obuf)
        lax.fori_loop(0, n // 2, step, 0)
        norm = obuf[pl.ds(9, rows, stride=16), :]
        motion = []
        for c in range(3):
            v = obuf[pl.ds(3 * c, rows, stride=16), :]
            v = v + obuf[pl.ds(3 * c + 1, rows, stride=16), :]
            v = v + obuf[pl.ds(3 * c + 2, rows, stride=16), :]
            motion.append(v / norm)
        if r < SMOOTH:
            store_motion(motion)
    mine = slice(FRONT, FRONT + nblk)
    mass = sums[0, mine, :]
    cross = jnp.zeros((nblk, 128), F32)
    energy = jnp.zeros((nblk, 128), F32)
    for c in range(3):
        m = motion[c][mine]
        out[c] = m
        cross = cross + sums[1 + c, mine, :] * m
        energy = energy + m * m
    stats[0:1, :] = jnp.sum(cross, axis=0, keepdims=True)
    stats[1:2, :] = jnp.sum(mass * energy, axis=0, keepdims=True)


def halo(first, last, axis):
    size = lax.axis_size(axis)
    up = [(i, i + 1) for i in range(size - 1)]
    down = [(i + 1, i) for i in range(size - 1)]
    return lax.ppermute(last, axis, up), lax.ppermute(first, axis, down)


def body(points, centroids, pair_blocks, pair_count, centroid_nbrs, sigma2):
    index_here = lax.axis_index("cells")
    nblk = centroids.shape[1] // 128
    pblk = points.shape[1] // 128
    nslot, nnbr = pair_blocks.shape[1], centroid_nbrs.shape[1]
    per_home = pblk // nblk
    ch = H * per_home
    nchunk = nblk // H
    rows = nblk + 2 * FRONT
    base = index_here * nblk
    pts = points.reshape(3, pblk, 128)
    cen = centroids.reshape(3, nblk, 128)
    before, after = halo(cen[:, :HALO], cen[:, nblk - HALO :], "cells")
    ext = jnp.concatenate([before, cen, after], axis=1)
    nbr_before, nbr_after = halo(
        centroid_nbrs[:FRONT], centroid_nbrs[nblk - FRONT :], "cells"
    )
    nbrs = jnp.concatenate([nbr_before, centroid_nbrs, nbr_after], axis=0) - (base - FRONT)
    lists = (pair_blocks - (base - REACH)).reshape(-1)
    totals = jnp.sum(pair_count.reshape(nchunk, ch), axis=1)
    start = jnp.reshape(base, (1,)).astype(jnp.int32)
    smem = pl.BlockSpec(memory_space=pltpu.SMEM)
    vmem = pl.BlockSpec(memory_space=pltpu.VMEM)
    most = ch * nslot + UNROLL
    crows = nblk + WIN - H
    features = [
        pltpu.VMEM((ch * KF, 128), F32),
        pltpu.VMEM((ch * KF, 128), F32),
        pltpu.VMEM((WIN * KF, 128), F32),
        pltpu.VMEM((WIN, 128, KF), BF16),
    ]
    params = pltpu.CompilerParams(vmem_limit_bytes=50 * 1024 * 1024)
    sums, stats = pl.pallas_call(
        functools.partial(pair_kernel, nslot, per_home, nchunk),
        out_shape=(
            jax.ShapeDtypeStruct((4, crows, 128), F32),
            jax.ShapeDtypeStruct((2, 128), F32),
        ),
        in_specs=[smem] * 5 + [vmem] * 2,
        out_specs=(vmem, vmem),
        scratch_shapes=features
        + [
            pltpu.VMEM((most, 128, 128), BF16),
            pltpu.VMEM((ch * 8, 128), F32),
            pltpu.VMEM((ch * 16, 128), F32),
            pltpu.VMEM((WIN * 16, 128), F32),
            pltpu.SMEM((most,), jnp.int32),
            pltpu.SMEM((most,), jnp.int32),
        ],
        compiler_params=params,
        name="pairs",
    )(
        lists, pair_count, totals, start, sigma2, pts,
        ext[:, HALO - REACH : HALO - REACH + crows],
    )
    sums = sums[:, : nblk + 2 * REACH]
    reach = FRONT + REACH
    from_left, from_right = halo(sums[:, :reach], sums[:, nblk + 2 * REACH - reach :], "cells")
    zeros = FRONT - REACH
    whole = jnp.pad(sums, ((0, 0), (zeros, zeros), (0, 0)))
    pad = rows - reach
    whole = whole + jnp.pad(from_left, ((0, 0), (0, pad), (0, 0)))
    whole = whole + jnp.pad(from_right, ((0, 0), (pad, 0), (0, 0)))
    off = HALO - FRONT
    motion, more = pl.pallas_call(
        functools.partial(smooth_kernel, nblk, nnbr),
        out_shape=(
            jax.ShapeDtypeStruct((3, nblk, 128), F32),
            jax.ShapeDtypeStruct((2, 128), F32),
        ),
        in_specs=[smem] * 2 + [vmem] * 3,
        out_specs=(vmem, vmem),
        scratch_shapes=[
            pltpu.VMEM((H * KF, 128), F32),
            pltpu.VMEM((H * KF, 128), F32),
            pltpu.VMEM((WIN * KF, 128), F32),
            pltpu.VMEM((WIN, 128, KF), BF16),
            pltpu.VMEM((rows, 128 * nnbr, 128), BF16),
            pltpu.VMEM((rows * 16, 128), F32),
            pltpu.VMEM((rows * 16, 128), F32),
        ],
        compiler_params=params,
        name="smoothing",
    )(
        nbrs.reshape(-1), start - FRONT, whole, ext[:, off : off + rows],
        ext[:, off - REACH : off - REACH + rows - H + WIN],
    )
    totals4 = lax.psum(jnp.concatenate([stats, more]), "cells")
    spread, count, cross, energy = [jnp.sum(totals4[i]) for i in range(4)]
    sigma_new = (spread - 2.0 * cross + energy) / (3.0 * count)
    return (motion.reshape(3, nblk * 128), jnp.reshape(sigma_new, (1,)))


def solution(mesh):
    return jax.shard_map(
        body,
        mesh=mesh,
        in_specs=(
            P(None, ("groups", "cells")),
            P(None, ("groups", "cells")),
            P(("groups", "cells"), None),
            P(("groups", "cells")),
            P(("groups", "cells"), None),
            P("groups"),
        ),
        out_specs=(P(None, ("groups", "cells")), P("groups")),
        check_vma=False,
    )
```

```python
import functools
import math

import jax
import jax.numpy as jnp
from jax import lax
from jax.experimental import pallas as pl
from jax.experimental.pallas import tpu as pltpu
from jax.sharding import PartitionSpec as P

REACH = 3
SMOOTH = 4
OUTLIER = 0.2
SHRINK = 1.0
KERNEL_VAR = 0.5
LOG2E = 1.4426950408889634

F32, BF16 = jnp.float32, jnp.bfloat16
KF = 32
H = 16
WIN = 24
DUMMY = WIN - 1
UNROLL = 32
HALO = 24
FRONT = 16


def split3(v):
    high = v.astype(BF16).astype(F32)
    rest = v - high
    mid = rest.astype(BF16).astype(F32)
    return high, mid, rest - mid


def lane_features(ref_a, ref_z, x, y, z, scale, root):
    rows = x.shape[0]
    ones = jnp.ones_like(x)
    x1, x2, x3 = split3(x)
    y1, y2, y3 = split3(y)
    own = split3(-scale * (x * x + y * y))
    height = split3(-root * z)
    half_a = [x1, x2, x1, x2, x3, x1, y1, y2, y1, y2, y3, y1, ones, ones, ones, *own]
    for k, v in enumerate(half_a):
        ref_a[pl.ds(k, rows, stride=KF), :] = v
    for k, v in enumerate([*height, ones, ones, ones]):
        ref_z[pl.ds(15 + k, rows, stride=KF), :] = v


def row_features(ref_t, x, y, z, scale, root, dead=None):
    rows = x.shape[0]
    ones = jnp.ones_like(x)
    x1, x2, x3 = split3(2.0 * scale * x)
    y1, y2, y3 = split3(2.0 * scale * y)
    own = -scale * (x * x + y * y)
    if dead is not None:
        own = jnp.where(dead, -1e9, own)
    feats = [x1, x1, x2, x2, x1, x3, y1, y1, y2, y2, y1, y3, *split3(own), ones, ones, ones]
    for k, v in enumerate(feats + list(split3(root * z))):
        ref_t[pl.ds(k, rows, stride=KF), :] = v


def transpose_features(ref_t, table):
    def step(i, carry):
        for u in range(8):
            j = i * 8 + u
            block = ref_t[pl.ds(pl.multiple_of(j * KF, KF), KF), :]
            table[j] = block.T.astype(BF16)
        return carry

    lax.fori_loop(0, WIN // 8, step, 0)


def pair_weights(table, ref_a, ref_z, l, b):
    at = pl.ds(pl.multiple_of(b * KF, KF), KF)
    right = jnp.concatenate([ref_a[at, :].astype(BF16), ref_z[at, :].astype(BF16)], axis=1)
    d = jnp.dot(table[l], right, preferred_element_type=F32)
    dz = d[:, 128:]
    return jnp.exp2(d[:, :128] - dz * dz)


def pair_kernel(
    nslot, per_home, nchunk, lists, counts, totals, first, sigma2, pts, cen,
    sums, stats, ref_a, ref_z, ref_t, table, wbuf, wacc, rbuf, acc, bsel, lsel,
):
    ch = H * per_home
    var = sigma2[0]
    scale_v = LOG2E / (2.0 * jnp.full((1, 128), var, F32))
    root_v = jnp.sqrt(scale_v)
    base_v = 2.0 * math.pi * jnp.full((1, 128), var, F32)
    outlier = base_v * jnp.sqrt(base_v) * (OUTLIER / (1.0 - OUTLIER) / per_home)
    for ref in (ref_a, ref_z, ref_t, rbuf):
        ref[...] = jnp.zeros_like(ref)
    sums[...] = jnp.zeros_like(sums)

    def chunk(ck, carry):
        spread, count = carry
        prow = pl.ds(pl.multiple_of(ck * ch, ch), ch)
        crow = pl.ds(pl.multiple_of(ck * H, H), WIN)
        origin = (first[0] + ck * H + H // 2).astype(F32)
        px, py = pts[0, prow, :] - origin, pts[1, prow, :]
        cx, cy = cen[0, crow, :] - origin, cen[1, crow, :]
        z0 = pts[2, pl.ds(pl.multiple_of(ck * ch, ch), 8), :][0:1, 0:1]
        pz = pts[2, prow, :] - z0
        cz = cen[2, crow, :] - z0
        lane_features(ref_a, ref_z, px, py, pz, scale_v, root_v)
        dead = lax.broadcasted_iota(jnp.int32, (WIN, 128), 0) == DUMMY
        row_features(ref_t, cx, cy, cz, scale_v, root_v, dead)
        transpose_features(ref_t, table)
        wacc[...] = jnp.zeros_like(wacc)
        acc[...] = jnp.zeros_like(acc)
        total = totals[ck]
        steps = (total + UNROLL - 1) // UNROLL

        def first_pass(i, state):
            b, s = state
            for u in range(UNROLL):
                k = i * UNROLL + u
                bb = jnp.minimum(b, ch - 1)
                at = ck * ch + bb
                l = lists[at * nslot + s] - ck * H
                l = jnp.where(k < total, l, DUMMY)
                bsel[k] = bb
                lsel[k] = l
                w = pair_weights(table, ref_a, ref_z, l, bb)
                wbuf[k] = w.astype(BF16)
                wrow = pl.ds(pl.multiple_of(bb * 8, 8), 8)
                wacc[wrow, :] += jnp.sum(w.reshape(16, 8, 128), axis=0)
                more = s + 1 < counts[at]
                b = jnp.where(more, b, b + 1)
                s = jnp.where(more, s + 1, 0)
            return b, s

        lax.fori_loop(0, steps, first_pass, (jnp.int32(0), jnp.int32(0)))
        weight = wacc[pl.ds(0, ch, stride=8), :]
        for i in range(1, 8):
            weight = weight + wacc[pl.ds(i, ch, stride=8), :]
        inv = 1.0 / (weight + outlier)
        count = count + weight * inv
        square = px * px + py * py + pz * pz
        feats = [inv, inv * px, inv * py, inv * pz, inv * square]
        for k, v in enumerate(feats):
            for t, piece in enumerate(split3(v)):
                rbuf[pl.ds(3 * k + t, ch, stride=16), :] = piece

        def second_pass(i, carry):
            for u in range(UNROLL):
                k = i * UNROLL + u
                b, l = bsel[k], lsel[k]
                r = rbuf[pl.ds(pl.multiple_of(b * 16, 16), 16), :].astype(BF16)
                o = lax.dot_general(
                    r, wbuf[k], (((1,), (1,)), ((), ())), preferred_element_type=F32
                )
                arow = pl.ds(pl.multiple_of(l * 16, 16), 16)
                acc[arow, :] += o
            return carry

        lax.fori_loop(0, steps, second_pass, 0)
        got = []
        for k in range(5):
            v = acc[pl.ds(3 * k, WIN, stride=16), :]
            v = v + acc[pl.ds(3 * k + 1, WIN, stride=16), :]
            got.append(v + acc[pl.ds(3 * k + 2, WIN, stride=16), :])
        mass, sx, sy, sz, sq = got
        pull_x, pull_y, pull_z = sx - cx * mass, sy - cy * mass, sz - cz * mass
        term = sq - (cx * sx + cy * sy + cz * sz) - (cx * pull_x + cy * pull_y + cz * pull_z)
        spread = spread + jnp.where(dead, 0.0, term)
        for k, v in enumerate([mass, pull_x, pull_y, pull_z]):
            sums[k, crow, :] += jnp.where(dead, 0.0, v)
        return spread, count

    init = (jnp.zeros((WIN, 128), F32), jnp.zeros((ch, 128), F32))
    spread, count = lax.fori_loop(0, nchunk, chunk, init)
    stats[0:1, :] = jnp.sum(spread, axis=0, keepdims=True)
    stats[1:2, :] = jnp.sum(count, axis=0, keepdims=True)


def smooth_kernel(
    nblk, nnbr, nbrs, first, sums, own, win, out, stats,
    ref_a, ref_z, ref_t, table, kern, mrow, obuf,
):
    rows = own.shape[1]
    scale = LOG2E / (2.0 * KERNEL_VAR)
    root = math.sqrt(scale)
    for ref in (ref_a, ref_z, ref_t, mrow):
        ref[...] = jnp.zeros_like(ref)
    mrow[pl.ds(9, rows, stride=16), :] = jnp.ones((rows, 128), F32)

    def chunk(ck, carry):
        orow = pl.ds(pl.multiple_of(ck * H, H), H)
        wrow = pl.ds(pl.multiple_of(ck * H, H), WIN)
        origin = (first[0] + ck * H + H // 2).astype(F32)
        z0 = own[2, pl.ds(pl.multiple_of(ck * H, H), 8), :][0:1, 0:1]
        lane_features(
            ref_a, ref_z, own[0, orow, :] - origin, own[1, orow, :], own[2, orow, :] - z0,
            scale, root,
        )
        row_features(
            ref_t, win[0, wrow, :] - origin, win[1, wrow, :], win[2, wrow, :] - z0, scale, root
        )
        transpose_features(ref_t, table)

        def step(i, carry):
            for j in range(8):
                b = i * 8 + j
                at = ck * H + b
                for s in range(nnbr):
                    l = nbrs[at * nnbr + s] - (ck * H - REACH)
                    l = jnp.clip(l, 0, WIN - 1)
                    w = pair_weights(table, ref_a, ref_z, l, b)
                    kern[at, s * 128 : (s + 1) * 128, :] = w.astype(BF16)
            return carry

        lax.fori_loop(0, H // 8, step, 0)
        return carry

    lax.fori_loop(0, rows // H, chunk, 0)

    def store_motion(motion):
        for k, v in enumerate(motion):
            for t, piece in enumerate(split3(v)):
                mrow[pl.ds(3 * k + t, rows, stride=16), :] = piece

    store_motion([sums[1 + c] / (sums[0] + SHRINK) for c in range(3)])
    for r in range(1, SMOOTH + 1):
        lo = FRONT - REACH * (SMOOTH - r)
        n = nblk + 2 * REACH * (SMOOTH - r)

        def step(i, carry):
            for u in range(8):
                at = lo + i * 8 + u
                left = []
                for s in range(nnbr):
                    j = jnp.clip(nbrs[at * nnbr + s], 0, rows - 1)
                    left.append(mrow[pl.ds(pl.multiple_of(j * 16, 16), 16), :].astype(BF16))
                o = jnp.dot(
                    jnp.concatenate(left, axis=1), kern[at], preferred_element_type=F32
                )
                obuf[pl.ds(pl.multiple_of(at * 16, 16), 16), :] = o
            return carry

        if r == 1:
            obuf[...] = jnp.ones_like(obuf)
        lax.fori_loop(0, (n + 7) // 8, step, 0)
        norm = obuf[pl.ds(9, rows, stride=16), :]
        motion = []
        for c in range(3):
            v = obuf[pl.ds(3 * c, rows, stride=16), :]
            v = v + obuf[pl.ds(3 * c + 1, rows, stride=16), :]
            v = v + obuf[pl.ds(3 * c + 2, rows, stride=16), :]
            motion.append(v / norm)
        if r < SMOOTH:
            store_motion(motion)
    mine = slice(FRONT, FRONT + nblk)
    mass = sums[0, mine, :]
    cross = jnp.zeros((nblk, 128), F32)
    energy = jnp.zeros((nblk, 128), F32)
    for c in range(3):
        m = motion[c][mine]
        out[c] = m
        cross = cross + sums[1 + c, mine, :] * m
        energy = energy + m * m
    stats[0:1, :] = jnp.sum(cross, axis=0, keepdims=True)
    stats[1:2, :] = jnp.sum(mass * energy, axis=0, keepdims=True)


def halo(first, last, axis):
    size = lax.axis_size(axis)
    up = [(i, i + 1) for i in range(size - 1)]
    down = [(i + 1, i) for i in range(size - 1)]
    return lax.ppermute(last, axis, up), lax.ppermute(first, axis, down)


def body(points, centroids, pair_blocks, pair_count, centroid_nbrs, sigma2):
    index_here = lax.axis_index("cells")
    nblk = centroids.shape[1] // 128
    pblk = points.shape[1] // 128
    nslot, nnbr = pair_blocks.shape[1], centroid_nbrs.shape[1]
    per_home = pblk // nblk
    ch = H * per_home
    nchunk = nblk // H
    rows = nblk + 2 * FRONT
    base = index_here * nblk
    pts = points.reshape(3, pblk, 128)
    cen = centroids.reshape(3, nblk, 128)
    before, after = halo(cen[:, :HALO], cen[:, nblk - HALO :], "cells")
    ext = jnp.concatenate([before, cen, after], axis=1)
    nbr_before, nbr_after = halo(
        centroid_nbrs[:FRONT], centroid_nbrs[nblk - FRONT :], "cells"
    )
    nbrs = jnp.concatenate([nbr_before, centroid_nbrs, nbr_after], axis=0) - (base - FRONT)
    lists = (pair_blocks - (base - REACH)).reshape(-1)
    totals = jnp.sum(pair_count.reshape(nchunk, ch), axis=1)
    start = jnp.reshape(base, (1,)).astype(jnp.int32)
    smem = pl.BlockSpec(memory_space=pltpu.SMEM)
    vmem = pl.BlockSpec(memory_space=pltpu.VMEM)
    most = ch * nslot + UNROLL
    crows = nblk + WIN - H
    features = [
        pltpu.VMEM((ch * KF, 128), F32),
        pltpu.VMEM((ch * KF, 128), F32),
        pltpu.VMEM((WIN * KF, 128), F32),
        pltpu.VMEM((WIN, 128, KF), BF16),
    ]
    params = pltpu.CompilerParams(vmem_limit_bytes=50 * 1024 * 1024)
    sums, stats = pl.pallas_call(
        functools.partial(pair_kernel, nslot, per_home, nchunk),
        out_shape=(
            jax.ShapeDtypeStruct((4, crows, 128), F32),
            jax.ShapeDtypeStruct((2, 128), F32),
        ),
        in_specs=[smem] * 5 + [vmem] * 2,
        out_specs=(vmem, vmem),
        scratch_shapes=features
        + [
            pltpu.VMEM((most, 128, 128), BF16),
            pltpu.VMEM((ch * 8, 128), F32),
            pltpu.VMEM((ch * 16, 128), F32),
            pltpu.VMEM((WIN * 16, 128), F32),
            pltpu.SMEM((most,), jnp.int32),
            pltpu.SMEM((most,), jnp.int32),
        ],
        compiler_params=params,
        name="pairs",
    )(
        lists, pair_count, totals, start, sigma2, pts,
        ext[:, HALO - REACH : HALO - REACH + crows],
    )
    sums = sums[:, : nblk + 2 * REACH]
    reach = FRONT + REACH
    from_left, from_right = halo(sums[:, :reach], sums[:, nblk + 2 * REACH - reach :], "cells")
    zeros = FRONT - REACH
    whole = jnp.pad(sums, ((0, 0), (zeros, zeros), (0, 0)))
    pad = rows - reach
    whole = whole + jnp.pad(from_left, ((0, 0), (0, pad), (0, 0)))
    whole = whole + jnp.pad(from_right, ((0, 0), (pad, 0), (0, 0)))
    off = HALO - FRONT
    motion, more = pl.pallas_call(
        functools.partial(smooth_kernel, nblk, nnbr),
        out_shape=(
            jax.ShapeDtypeStruct((3, nblk, 128), F32),
            jax.ShapeDtypeStruct((2, 128), F32),
        ),
        in_specs=[smem] * 2 + [vmem] * 3,
        out_specs=(vmem, vmem),
        scratch_shapes=[
            pltpu.VMEM((H * KF, 128), F32),
            pltpu.VMEM((H * KF, 128), F32),
            pltpu.VMEM((WIN * KF, 128), F32),
            pltpu.VMEM((WIN, 128, KF), BF16),
            pltpu.VMEM((rows, 128 * nnbr, 128), BF16),
            pltpu.VMEM((rows * 16, 128), F32),
            pltpu.VMEM((rows * 16, 128), F32),
        ],
        compiler_params=params,
        name="smoothing",
    )(
        nbrs.reshape(-1), start - FRONT, whole, ext[:, off : off + rows],
        ext[:, off - REACH : off - REACH + rows - H + WIN],
    )
    totals4 = lax.psum(jnp.concatenate([stats, more]), "cells")
    spread, count, cross, energy = [jnp.sum(totals4[i]) for i in range(4)]
    sigma_new = (spread - 2.0 * cross + energy) / (3.0 * count)
    return (motion.reshape(3, nblk * 128), jnp.reshape(sigma_new, (1,)))


def solution(mesh):
    return jax.shard_map(
        body,
        mesh=mesh,
        in_specs=(
            P(None, ("groups", "cells")),
            P(None, ("groups", "cells")),
            P(("groups", "cells"), None),
            P(("groups", "cells")),
            P(("groups", "cells"), None),
            P("groups"),
        ),
        out_specs=(P(None, ("groups", "cells")), P("groups")),
        check_vma=False,
    )
```

```python
import functools
import math

import jax
import jax.numpy as jnp
from jax import lax
from jax.experimental import pallas as pl
from jax.experimental.pallas import tpu as pltpu
from jax.sharding import PartitionSpec as P

REACH = 3
SMOOTH = 4
OUTLIER = 0.2
SHRINK = 1.0
KERNEL_VAR = 0.5
LOG2E = 1.4426950408889634

F32, BF16 = jnp.float32, jnp.bfloat16
KF = 32
H = 16
WIN = 24
DUMMY = WIN - 1
UNROLL = 32
HALO = 24
FRONT = 16


def split3(v):
    high = v.astype(BF16).astype(F32)
    rest = v - high
    mid = rest.astype(BF16).astype(F32)
    return high, mid, rest - mid


def lane_features(ref_a, ref_z, x, y, z, scale, root):
    rows = x.shape[0]
    ones = jnp.ones_like(x)
    x1, x2, x3 = split3(x)
    y1, y2, y3 = split3(y)
    own = split3(-scale * (x * x + y * y))
    height = split3(-root * z)
    half_a = [x1, x2, x1, x2, x3, x1, y1, y2, y1, y2, y3, y1, ones, ones, ones, *own]
    for k, v in enumerate(half_a):
        ref_a[pl.ds(k, rows, stride=KF), :] = v
    for k, v in enumerate([*height, ones, ones, ones]):
        ref_z[pl.ds(15 + k, rows, stride=KF), :] = v


def row_features(ref_t, x, y, z, scale, root, dead=None):
    rows = x.shape[0]
    ones = jnp.ones_like(x)
    x1, x2, x3 = split3(2.0 * scale * x)
    y1, y2, y3 = split3(2.0 * scale * y)
    own = -scale * (x * x + y * y)
    if dead is not None:
        own = jnp.where(dead, -1e9, own)
    feats = [x1, x1, x2, x2, x1, x3, y1, y1, y2, y2, y1, y3, *split3(own), ones, ones, ones]
    for k, v in enumerate(feats + list(split3(root * z))):
        ref_t[pl.ds(k, rows, stride=KF), :] = v


def transpose_features(ref_t, table):
    def step(i, carry):
        for u in range(8):
            j = i * 8 + u
            block = ref_t[pl.ds(pl.multiple_of(j * KF, KF), KF), :]
            table[j] = block.T.astype(BF16)
        return carry

    lax.fori_loop(0, WIN // 8, step, 0)


def pair_weights(table, ref_a, ref_z, l, b):
    at = pl.ds(pl.multiple_of(b * KF, KF), KF)
    right = jnp.concatenate([ref_a[at, :].astype(BF16), ref_z[at, :].astype(BF16)], axis=1)
    d = jnp.dot(table[l], right, preferred_element_type=F32)
    dz = d[:, 128:]
    return jnp.exp2(d[:, :128] - dz * dz)


def pair_kernel(
    nslot, per_home, nchunk, lists, counts, totals, first, sigma2, pts, cen,
    sums, stats, ref_a, ref_z, ref_t, table, wbuf, wacc, rbuf, acc, bsel, lsel,
):
    ch = H * per_home
    var = sigma2[0]
    scale_v = LOG2E / (2.0 * jnp.full((1, 128), var, F32))
    root_v = jnp.sqrt(scale_v)
    base_v = 2.0 * math.pi * jnp.full((1, 128), var, F32)
    outlier = base_v * jnp.sqrt(base_v) * (OUTLIER / (1.0 - OUTLIER) / per_home)
    for ref in (ref_a, ref_z, ref_t, rbuf):
        ref[...] = jnp.zeros_like(ref)
    sums[...] = jnp.zeros_like(sums)

    def chunk(ck, carry):
        spread, count = carry
        prow = pl.ds(pl.multiple_of(ck * ch, ch), ch)
        crow = pl.ds(pl.multiple_of(ck * H, H), WIN)
        origin = (first[0] + ck * H + H // 2).astype(F32)
        px, py = pts[0, prow, :] - origin, pts[1, prow, :]
        cx, cy = cen[0, crow, :] - origin, cen[1, crow, :]
        z0 = pts[2, pl.ds(pl.multiple_of(ck * ch, ch), 8), :][0:1, 0:1]
        pz = pts[2, prow, :] - z0
        cz = cen[2, crow, :] - z0
        lane_features(ref_a, ref_z, px, py, pz, scale_v, root_v)
        dead = lax.broadcasted_iota(jnp.int32, (WIN, 128), 0) == DUMMY
        row_features(ref_t, cx, cy, cz, scale_v, root_v, dead)
        transpose_features(ref_t, table)
        wacc[...] = jnp.zeros_like(wacc)
        acc[...] = jnp.zeros_like(acc)
        total = totals[ck]
        steps = (total + UNROLL - 1) // UNROLL

        def first_pass(i, state):
            b, s = state
            for u in range(UNROLL):
                k = i * UNROLL + u
                bb = jnp.minimum(b, ch - 1)
                at = ck * ch + bb
                l = lists[at * nslot + s] - ck * H
                l = jnp.where(k < total, l, DUMMY)
                bsel[k] = bb
                lsel[k] = l
                w = pair_weights(table, ref_a, ref_z, l, bb)
                wbuf[k] = w.astype(BF16)
                wrow = pl.ds(pl.multiple_of(bb * 8, 8), 8)
                wacc[wrow, :] += jnp.sum(w.reshape(16, 8, 128), axis=0)
                more = s + 1 < counts[at]
                b = jnp.where(more, b, b + 1)
                s = jnp.where(more, s + 1, 0)
            return b, s

        lax.fori_loop(0, steps, first_pass, (jnp.int32(0), jnp.int32(0)))
        weight = wacc[pl.ds(0, ch, stride=8), :]
        for i in range(1, 8):
            weight = weight + wacc[pl.ds(i, ch, stride=8), :]
        inv = 1.0 / (weight + outlier)
        count = count + weight * inv
        square = px * px + py * py + pz * pz
        feats = [inv, inv * px, inv * py, inv * pz, inv * square]
        for k, v in enumerate(feats):
            for t, piece in enumerate(split3(v)):
                rbuf[pl.ds(3 * k + t, ch, stride=16), :] = piece

        def second_pass(i, carry):
            for u in range(UNROLL):
                k = i * UNROLL + u
                b, l = bsel[k], lsel[k]
                r = rbuf[pl.ds(pl.multiple_of(b * 16, 16), 16), :].astype(BF16)
                o = lax.dot_general(
                    r, wbuf[k], (((1,), (1,)), ((), ())), preferred_element_type=F32
                )
                arow = pl.ds(pl.multiple_of(l * 16, 16), 16)
                acc[arow, :] += o
            return carry

        lax.fori_loop(0, steps, second_pass, 0)
        got = []
        for k in range(5):
            v = acc[pl.ds(3 * k, WIN, stride=16), :]
            v = v + acc[pl.ds(3 * k + 1, WIN, stride=16), :]
            got.append(v + acc[pl.ds(3 * k + 2, WIN, stride=16), :])
        mass, sx, sy, sz, sq = got
        pull_x, pull_y, pull_z = sx - cx * mass, sy - cy * mass, sz - cz * mass
        term = sq - (cx * sx + cy * sy + cz * sz) - (cx * pull_x + cy * pull_y + cz * pull_z)
        spread = spread + jnp.where(dead, 0.0, term)
        for k, v in enumerate([mass, pull_x, pull_y, pull_z]):
            sums[k, crow, :] += jnp.where(dead, 0.0, v)
        return spread, count

    init = (jnp.zeros((WIN, 128), F32), jnp.zeros((ch, 128), F32))
    spread, count = lax.fori_loop(0, nchunk, chunk, init)
    stats[0:1, :] = jnp.sum(spread, axis=0, keepdims=True)
    stats[1:2, :] = jnp.sum(count, axis=0, keepdims=True)


def smooth_kernel(
    nblk, nnbr, nbrs, first, sums, own, win, out, stats,
    ref_a, ref_z, ref_t, table, kern, mrow, obuf,
):
    rows = own.shape[1]
    scale = LOG2E / (2.0 * KERNEL_VAR)
    root = math.sqrt(scale)
    for ref in (ref_a, ref_z, ref_t, mrow):
        ref[...] = jnp.zeros_like(ref)
    mrow[pl.ds(9, rows, stride=16), :] = jnp.ones((rows, 128), F32)

    def chunk(ck, carry):
        orow = pl.ds(pl.multiple_of(ck * H, H), H)
        wrow = pl.ds(pl.multiple_of(ck * H, H), WIN)
        origin = (first[0] + ck * H + H // 2).astype(F32)
        z0 = own[2, pl.ds(pl.multiple_of(ck * H, H), 8), :][0:1, 0:1]
        lane_features(
            ref_a, ref_z, own[0, orow, :] - origin, own[1, orow, :], own[2, orow, :] - z0,
            scale, root,
        )
        row_features(
            ref_t, win[0, wrow, :] - origin, win[1, wrow, :], win[2, wrow, :] - z0, scale, root
        )
        transpose_features(ref_t, table)

        def step(i, carry):
            for j in range(8):
                b = i * 8 + j
                at = ck * H + b
                for s in range(nnbr):
                    l = nbrs[at * nnbr + s] - (ck * H - REACH)
                    l = jnp.clip(l, 0, WIN - 1)
                    w = pair_weights(table, ref_a, ref_z, l, b)
                    kern[at, s * 128 : (s + 1) * 128, :] = w.astype(BF16)
            return carry

        lax.fori_loop(0, H // 8, step, 0)
        return carry

    lax.fori_loop(0, rows // H, chunk, 0)

    def store_motion(motion):
        for k, v in enumerate(motion):
            for t, piece in enumerate(split3(v)):
                mrow[pl.ds(3 * k + t, rows, stride=16), :] = piece

    store_motion([sums[1 + c] / (sums[0] + SHRINK) for c in range(3)])
    for r in range(1, SMOOTH + 1):
        lo = FRONT - REACH * (SMOOTH - r)
        n = nblk + 2 * REACH * (SMOOTH - r)

        def step(i, carry):
            for u in range(8):
                at = lo + i * 8 + u
                left = []
                for s in range(nnbr):
                    j = jnp.clip(nbrs[at * nnbr + s], 0, rows - 1)
                    left.append(mrow[pl.ds(pl.multiple_of(j * 16, 16), 16), :].astype(BF16))
                o = jnp.dot(
                    jnp.concatenate(left, axis=1), kern[at], preferred_element_type=F32
                )
                obuf[pl.ds(pl.multiple_of(at * 16, 16), 16), :] = o
            return carry

        if r == 1:
            obuf[...] = jnp.ones_like(obuf)
        lax.fori_loop(0, (n + 7) // 8, step, 0)
        norm = obuf[pl.ds(9, rows, stride=16), :]
        motion = []
        for c in range(3):
            v = obuf[pl.ds(3 * c, rows, stride=16), :]
            v = v + obuf[pl.ds(3 * c + 1, rows, stride=16), :]
            v = v + obuf[pl.ds(3 * c + 2, rows, stride=16), :]
            motion.append(v / norm)
        if r < SMOOTH:
            store_motion(motion)
    mine = slice(FRONT, FRONT + nblk)
    mass = sums[0, mine, :]
    cross = jnp.zeros((nblk, 128), F32)
    energy = jnp.zeros((nblk, 128), F32)
    for c in range(3):
        m = motion[c][mine]
        out[c] = m
        cross = cross + sums[1 + c, mine, :] * m
        energy = energy + m * m
    stats[0:1, :] = jnp.sum(cross, axis=0, keepdims=True)
    stats[1:2, :] = jnp.sum(mass * energy, axis=0, keepdims=True)


def halo(first, last, axis):
    size = lax.axis_size(axis)
    up = [(i, i + 1) for i in range(size - 1)]
    down = [(i + 1, i) for i in range(size - 1)]
    return lax.ppermute(last, axis, up), lax.ppermute(first, axis, down)


def axis_total(x, axis):
    size = lax.axis_size(axis)
    if size & (size - 1):
        return lax.psum(x, axis)
    step = 1
    while step < size:
        x = x + lax.ppermute(x, axis, [(i, i ^ step) for i in range(size)])
        step *= 2
    return x


def body(points, centroids, pair_blocks, pair_count, centroid_nbrs, sigma2):
    index_here = lax.axis_index("cells")
    nblk = centroids.shape[1] // 128
    pblk = points.shape[1] // 128
    nslot, nnbr = pair_blocks.shape[1], centroid_nbrs.shape[1]
    per_home = pblk // nblk
    ch = H * per_home
    nchunk = nblk // H
    rows = nblk + 2 * FRONT
    base = index_here * nblk
    pts = points.reshape(3, pblk, 128)
    cen = centroids.reshape(3, nblk, 128)
    before, after = halo(cen[:, :HALO], cen[:, nblk - HALO :], "cells")
    ext = jnp.concatenate([before, cen, after], axis=1)
    nbr_before, nbr_after = halo(
        centroid_nbrs[:FRONT], centroid_nbrs[nblk - FRONT :], "cells"
    )
    nbrs = jnp.concatenate([nbr_before, centroid_nbrs, nbr_after], axis=0) - (base - FRONT)
    lists = (pair_blocks - (base - REACH)).reshape(-1)
    totals = jnp.sum(pair_count.reshape(nchunk, ch), axis=1)
    start = jnp.reshape(base, (1,)).astype(jnp.int32)
    smem = pl.BlockSpec(memory_space=pltpu.SMEM)
    vmem = pl.BlockSpec(memory_space=pltpu.VMEM)
    most = ch * nslot + UNROLL
    crows = nblk + WIN - H
    features = [
        pltpu.VMEM((ch * KF, 128), F32),
        pltpu.VMEM((ch * KF, 128), F32),
        pltpu.VMEM((WIN * KF, 128), F32),
        pltpu.VMEM((WIN, 128, KF), BF16),
    ]
    params = pltpu.CompilerParams(vmem_limit_bytes=50 * 1024 * 1024)
    sums, stats = pl.pallas_call(
        functools.partial(pair_kernel, nslot, per_home, nchunk),
        out_shape=(
            jax.ShapeDtypeStruct((4, crows, 128), F32),
            jax.ShapeDtypeStruct((2, 128), F32),
        ),
        in_specs=[smem] * 5 + [vmem] * 2,
        out_specs=(vmem, vmem),
        scratch_shapes=features
        + [
            pltpu.VMEM((most, 128, 128), BF16),
            pltpu.VMEM((ch * 8, 128), F32),
            pltpu.VMEM((ch * 16, 128), F32),
            pltpu.VMEM((WIN * 16, 128), F32),
            pltpu.SMEM((most,), jnp.int32),
            pltpu.SMEM((most,), jnp.int32),
        ],
        compiler_params=params,
        name="pairs",
    )(
        lists, pair_count, totals, start, sigma2, pts,
        ext[:, HALO - REACH : HALO - REACH + crows],
    )
    sums = sums[:, : nblk + 2 * REACH]
    reach = FRONT + REACH
    from_left, from_right = halo(sums[:, :reach], sums[:, nblk + 2 * REACH - reach :], "cells")
    zeros = FRONT - REACH
    whole = jnp.pad(sums, ((0, 0), (zeros, zeros), (0, 0)))
    pad = rows - reach
    whole = whole + jnp.pad(from_left, ((0, 0), (0, pad), (0, 0)))
    whole = whole + jnp.pad(from_right, ((0, 0), (pad, 0), (0, 0)))
    off = HALO - FRONT
    motion, more = pl.pallas_call(
        functools.partial(smooth_kernel, nblk, nnbr),
        out_shape=(
            jax.ShapeDtypeStruct((3, nblk, 128), F32),
            jax.ShapeDtypeStruct((2, 128), F32),
        ),
        in_specs=[smem] * 2 + [vmem] * 3,
        out_specs=(vmem, vmem),
        scratch_shapes=[
            pltpu.VMEM((H * KF, 128), F32),
            pltpu.VMEM((H * KF, 128), F32),
            pltpu.VMEM((WIN * KF, 128), F32),
            pltpu.VMEM((WIN, 128, KF), BF16),
            pltpu.VMEM((rows, 128 * nnbr, 128), BF16),
            pltpu.VMEM((rows * 16, 128), F32),
            pltpu.VMEM((rows * 16, 128), F32),
        ],
        compiler_params=params,
        name="smoothing",
    )(
        nbrs.reshape(-1), start - FRONT, whole, ext[:, off : off + rows],
        ext[:, off - REACH : off - REACH + rows - H + WIN],
    )
    totals4 = axis_total(jnp.concatenate([stats, more]), "cells")
    spread, count, cross, energy = [jnp.sum(totals4[i]) for i in range(4)]
    sigma_new = (spread - 2.0 * cross + energy) / (3.0 * count)
    return (motion.reshape(3, nblk * 128), jnp.reshape(sigma_new, (1,)))


def solution(mesh):
    return jax.shard_map(
        body,
        mesh=mesh,
        in_specs=(
            P(None, ("groups", "cells")),
            P(None, ("groups", "cells")),
            P(("groups", "cells"), None),
            P(("groups", "cells")),
            P(("groups", "cells"), None),
            P("groups"),
        ),
        out_specs=(P(None, ("groups", "cells")), P("groups")),
        check_vma=False,
    )
```

```python
import functools
import math

import jax
import jax.numpy as jnp
from jax import lax
from jax.experimental import pallas as pl
from jax.experimental.pallas import tpu as pltpu
from jax.sharding import PartitionSpec as P

REACH = 3
SMOOTH = 4
OUTLIER = 0.2
SHRINK = 1.0
KERNEL_VAR = 0.5
LOG2E = 1.4426950408889634

F32, BF16 = jnp.float32, jnp.bfloat16
KF = 32
H = 16
WIN = 24
DUMMY = WIN - 1
UNROLL = 64
HALO = 24
FRONT = 16


def split3(v):
    high = v.astype(BF16).astype(F32)
    rest = v - high
    mid = rest.astype(BF16).astype(F32)
    return high, mid, rest - mid


def lane_features(ref_a, ref_z, x, y, z, scale, root):
    rows = x.shape[0]
    ones = jnp.ones_like(x)
    x1, x2, x3 = split3(x)
    y1, y2, y3 = split3(y)
    own = split3(-scale * (x * x + y * y))
    height = split3(-root * z)
    half_a = [x1, x2, x1, x2, x3, x1, y1, y2, y1, y2, y3, y1, ones, ones, ones, *own]
    for k, v in enumerate(half_a):
        ref_a[pl.ds(k, rows, stride=KF), :] = v
    for k, v in enumerate([*height, ones, ones, ones]):
        ref_z[pl.ds(15 + k, rows, stride=KF), :] = v


def row_features(ref_t, x, y, z, scale, root, dead=None):
    rows = x.shape[0]
    ones = jnp.ones_like(x)
    x1, x2, x3 = split3(2.0 * scale * x)
    y1, y2, y3 = split3(2.0 * scale * y)
    own = -scale * (x * x + y * y)
    if dead is not None:
        own = jnp.where(dead, -1e9, own)
    feats = [x1, x1, x2, x2, x1, x3, y1, y1, y2, y2, y1, y3, *split3(own), ones, ones, ones]
    for k, v in enumerate(feats + list(split3(root * z))):
        ref_t[pl.ds(k, rows, stride=KF), :] = v


def transpose_features(ref_t, table):
    def step(i, carry):
        for u in range(8):
            j = i * 8 + u
            block = ref_t[pl.ds(pl.multiple_of(j * KF, KF), KF), :]
            table[j] = block.T.astype(BF16)
        return carry

    lax.fori_loop(0, WIN // 8, step, 0)


def pair_weights(table, ref_a, ref_z, l, b):
    at = pl.ds(pl.multiple_of(b * KF, KF), KF)
    right = jnp.concatenate([ref_a[at, :].astype(BF16), ref_z[at, :].astype(BF16)], axis=1)
    d = jnp.dot(table[l], right, preferred_element_type=F32)
    dz = d[:, 128:]
    return jnp.exp2(d[:, :128] - dz * dz)


def pair_kernel(
    nslot, per_home, nchunk, lists, counts, totals, first, sigma2, pts, cen,
    sums, stats, ref_a, ref_z, ref_t, table, wbuf, wacc, rbuf, acc, bsel, lsel,
):
    ch = H * per_home
    var = sigma2[0]
    scale_v = LOG2E / (2.0 * jnp.full((1, 128), var, F32))
    root_v = jnp.sqrt(scale_v)
    base_v = 2.0 * math.pi * jnp.full((1, 128), var, F32)
    outlier = base_v * jnp.sqrt(base_v) * (OUTLIER / (1.0 - OUTLIER) / per_home)
    for ref in (ref_a, ref_z, ref_t, rbuf):
        ref[...] = jnp.zeros_like(ref)
    sums[...] = jnp.zeros_like(sums)

    def chunk(ck, carry):
        spread, count = carry
        prow = pl.ds(pl.multiple_of(ck * ch, ch), ch)
        crow = pl.ds(pl.multiple_of(ck * H, H), WIN)
        origin = (first[0] + ck * H + H // 2).astype(F32)
        px, py = pts[0, prow, :] - origin, pts[1, prow, :]
        cx, cy = cen[0, crow, :] - origin, cen[1, crow, :]
        z0 = pts[2, pl.ds(pl.multiple_of(ck * ch, ch), 8), :][0:1, 0:1]
        pz = pts[2, prow, :] - z0
        cz = cen[2, crow, :] - z0
        lane_features(ref_a, ref_z, px, py, pz, scale_v, root_v)
        dead = lax.broadcasted_iota(jnp.int32, (WIN, 128), 0) == DUMMY
        row_features(ref_t, cx, cy, cz, scale_v, root_v, dead)
        transpose_features(ref_t, table)
        wacc[...] = jnp.zeros_like(wacc)
        acc[...] = jnp.zeros_like(acc)
        total = totals[ck]
        steps = (total + UNROLL - 1) // UNROLL

        def first_pass(i, state):
            b, s = state
            for u in range(UNROLL):
                k = i * UNROLL + u
                bb = jnp.minimum(b, ch - 1)
                at = ck * ch + bb
                l = lists[at * nslot + s] - ck * H
                l = jnp.where(k < total, l, DUMMY)
                bsel[k] = bb
                lsel[k] = l
                w = pair_weights(table, ref_a, ref_z, l, bb)
                wbuf[k] = w.astype(BF16)
                wrow = pl.ds(pl.multiple_of(bb * 8, 8), 8)
                wacc[wrow, :] += jnp.sum(w.reshape(16, 8, 128), axis=0)
                more = s + 1 < counts[at]
                b = jnp.where(more, b, b + 1)
                s = jnp.where(more, s + 1, 0)
            return b, s

        lax.fori_loop(0, steps, first_pass, (jnp.int32(0), jnp.int32(0)))
        weight = wacc[pl.ds(0, ch, stride=8), :]
        for i in range(1, 8):
            weight = weight + wacc[pl.ds(i, ch, stride=8), :]
        inv = 1.0 / (weight + outlier)
        count = count + weight * inv
        square = px * px + py * py + pz * pz
        feats = [inv, inv * px, inv * py, inv * pz, inv * square]
        for k, v in enumerate(feats):
            for t, piece in enumerate(split3(v)):
                rbuf[pl.ds(3 * k + t, ch, stride=16), :] = piece

        def second_pass(i, carry):
            for u in range(UNROLL):
                k = i * UNROLL + u
                b, l = bsel[k], lsel[k]
                r = rbuf[pl.ds(pl.multiple_of(b * 16, 16), 16), :].astype(BF16)
                o = lax.dot_general(
                    r, wbuf[k], (((1,), (1,)), ((), ())), preferred_element_type=F32
                )
                arow = pl.ds(pl.multiple_of(l * 16, 16), 16)
                acc[arow, :] += o
            return carry

        lax.fori_loop(0, steps, second_pass, 0)
        got = []
        for k in range(5):
            v = acc[pl.ds(3 * k, WIN, stride=16), :]
            v = v + acc[pl.ds(3 * k + 1, WIN, stride=16), :]
            got.append(v + acc[pl.ds(3 * k + 2, WIN, stride=16), :])
        mass, sx, sy, sz, sq = got
        pull_x, pull_y, pull_z = sx - cx * mass, sy - cy * mass, sz - cz * mass
        term = sq - (cx * sx + cy * sy + cz * sz) - (cx * pull_x + cy * pull_y + cz * pull_z)
        spread = spread + jnp.where(dead, 0.0, term)
        for k, v in enumerate([mass, pull_x, pull_y, pull_z]):
            sums[k, crow, :] += jnp.where(dead, 0.0, v)
        return spread, count

    init = (jnp.zeros((WIN, 128), F32), jnp.zeros((ch, 128), F32))
    spread, count = lax.fori_loop(0, nchunk, chunk, init)
    stats[0:1, :] = jnp.sum(spread, axis=0, keepdims=True)
    stats[1:2, :] = jnp.sum(count, axis=0, keepdims=True)


def smooth_kernel(
    nblk, nnbr, nbrs, first, sums, own, win, out, stats,
    ref_a, ref_z, ref_t, table, kern, mrow, obuf,
):
    rows = own.shape[1]
    scale = LOG2E / (2.0 * KERNEL_VAR)
    root = math.sqrt(scale)
    for ref in (ref_a, ref_z, ref_t, mrow):
        ref[...] = jnp.zeros_like(ref)
    mrow[pl.ds(9, rows, stride=16), :] = jnp.ones((rows, 128), F32)

    def chunk(ck, carry):
        orow = pl.ds(pl.multiple_of(ck * H, H), H)
        wrow = pl.ds(pl.multiple_of(ck * H, H), WIN)
        origin = (first[0] + ck * H + H // 2).astype(F32)
        z0 = own[2, pl.ds(pl.multiple_of(ck * H, H), 8), :][0:1, 0:1]
        lane_features(
            ref_a, ref_z, own[0, orow, :] - origin, own[1, orow, :], own[2, orow, :] - z0,
            scale, root,
        )
        row_features(
            ref_t, win[0, wrow, :] - origin, win[1, wrow, :], win[2, wrow, :] - z0, scale, root
        )
        transpose_features(ref_t, table)

        def step(i, carry):
            for j in range(H):
                b = i * H + j
                at = ck * H + b
                for s in range(nnbr):
                    l = nbrs[at * nnbr + s] - (ck * H - REACH)
                    l = jnp.clip(l, 0, WIN - 1)
                    w = pair_weights(table, ref_a, ref_z, l, b)
                    kern[at, s * 128 : (s + 1) * 128, :] = w.astype(BF16)
            return carry

        step(0, 0)
        return carry

    lax.fori_loop(0, rows // H, chunk, 0)

    def store_motion(motion):
        for k, v in enumerate(motion):
            for t, piece in enumerate(split3(v)):
                mrow[pl.ds(3 * k + t, rows, stride=16), :] = piece

    store_motion([sums[1 + c] / (sums[0] + SHRINK) for c in range(3)])
    for r in range(1, SMOOTH + 1):
        lo = FRONT - REACH * (SMOOTH - r)
        n = nblk + 2 * REACH * (SMOOTH - r)

        def step(i, carry):
            for u in range(8):
                at = lo + i * 8 + u
                left = []
                for s in range(nnbr):
                    j = jnp.clip(nbrs[at * nnbr + s], 0, rows - 1)
                    left.append(mrow[pl.ds(pl.multiple_of(j * 16, 16), 16), :].astype(BF16))
                o = jnp.dot(
                    jnp.concatenate(left, axis=1), kern[at], preferred_element_type=F32
                )
                obuf[pl.ds(pl.multiple_of(at * 16, 16), 16), :] = o
            return carry

        if r == 1:
            obuf[...] = jnp.ones_like(obuf)
        lax.fori_loop(0, (n + 7) // 8, step, 0)
        norm = obuf[pl.ds(9, rows, stride=16), :]
        motion = []
        for c in range(3):
            v = obuf[pl.ds(3 * c, rows, stride=16), :]
            v = v + obuf[pl.ds(3 * c + 1, rows, stride=16), :]
            v = v + obuf[pl.ds(3 * c + 2, rows, stride=16), :]
            motion.append(v / norm)
        if r < SMOOTH:
            store_motion(motion)
    mine = slice(FRONT, FRONT + nblk)
    mass = sums[0, mine, :]
    cross = jnp.zeros((nblk, 128), F32)
    energy = jnp.zeros((nblk, 128), F32)
    for c in range(3):
        m = motion[c][mine]
        out[c] = m
        cross = cross + sums[1 + c, mine, :] * m
        energy = energy + m * m
    stats[0:1, :] = jnp.sum(cross, axis=0, keepdims=True)
    stats[1:2, :] = jnp.sum(mass * energy, axis=0, keepdims=True)


def halo(first, last, axis):
    size = lax.axis_size(axis)
    up = [(i, i + 1) for i in range(size - 1)]
    down = [(i + 1, i) for i in range(size - 1)]
    return lax.ppermute(last, axis, up), lax.ppermute(first, axis, down)


def axis_total(x, axis):
    size = lax.axis_size(axis)
    if size & (size - 1):
        return lax.psum(x, axis)
    step = 1
    while step < size:
        x = x + lax.ppermute(x, axis, [(i, i ^ step) for i in range(size)])
        step *= 2
    return x


def body(points, centroids, pair_blocks, pair_count, centroid_nbrs, sigma2):
    index_here = lax.axis_index("cells")
    nblk = centroids.shape[1] // 128
    pblk = points.shape[1] // 128
    nslot, nnbr = pair_blocks.shape[1], centroid_nbrs.shape[1]
    per_home = pblk // nblk
    ch = H * per_home
    nchunk = nblk // H
    rows = nblk + 2 * FRONT
    base = index_here * nblk
    pts = points.reshape(3, pblk, 128)
    cen = centroids.reshape(3, nblk, 128)
    before, after = halo(cen[:, :HALO], cen[:, nblk - HALO :], "cells")
    ext = jnp.concatenate([before, cen, after], axis=1)
    nbr_before, nbr_after = halo(
        centroid_nbrs[:FRONT], centroid_nbrs[nblk - FRONT :], "cells"
    )
    nbrs = jnp.concatenate([nbr_before, centroid_nbrs, nbr_after], axis=0) - (base - FRONT)
    lists = (pair_blocks - (base - REACH)).reshape(-1)
    totals = jnp.sum(pair_count.reshape(nchunk, ch), axis=1)
    start = jnp.reshape(base, (1,)).astype(jnp.int32)
    smem = pl.BlockSpec(memory_space=pltpu.SMEM)
    vmem = pl.BlockSpec(memory_space=pltpu.VMEM)
    most = ch * nslot + UNROLL
    crows = nblk + WIN - H
    features = [
        pltpu.VMEM((ch * KF, 128), F32),
        pltpu.VMEM((ch * KF, 128), F32),
        pltpu.VMEM((WIN * KF, 128), F32),
        pltpu.VMEM((WIN, 128, KF), BF16),
    ]
    params = pltpu.CompilerParams(vmem_limit_bytes=50 * 1024 * 1024)
    sums, stats = pl.pallas_call(
        functools.partial(pair_kernel, nslot, per_home, nchunk),
        out_shape=(
            jax.ShapeDtypeStruct((4, crows, 128), F32),
            jax.ShapeDtypeStruct((2, 128), F32),
        ),
        in_specs=[smem] * 5 + [vmem] * 2,
        out_specs=(vmem, vmem),
        scratch_shapes=features
        + [
            pltpu.VMEM((most, 128, 128), BF16),
            pltpu.VMEM((ch * 8, 128), F32),
            pltpu.VMEM((ch * 16, 128), F32),
            pltpu.VMEM((WIN * 16, 128), F32),
            pltpu.SMEM((most,), jnp.int32),
            pltpu.SMEM((most,), jnp.int32),
        ],
        compiler_params=params,
        name="pairs",
    )(
        lists, pair_count, totals, start, sigma2, pts,
        ext[:, HALO - REACH : HALO - REACH + crows],
    )
    sums = sums[:, : nblk + 2 * REACH]
    reach = FRONT + REACH
    from_left, from_right = halo(sums[:, :reach], sums[:, nblk + 2 * REACH - reach :], "cells")
    zeros = FRONT - REACH
    whole = jnp.pad(sums, ((0, 0), (zeros, zeros), (0, 0)))
    pad = rows - reach
    whole = whole + jnp.pad(from_left, ((0, 0), (0, pad), (0, 0)))
    whole = whole + jnp.pad(from_right, ((0, 0), (pad, 0), (0, 0)))
    off = HALO - FRONT
    motion, more = pl.pallas_call(
        functools.partial(smooth_kernel, nblk, nnbr),
        out_shape=(
            jax.ShapeDtypeStruct((3, nblk, 128), F32),
            jax.ShapeDtypeStruct((2, 128), F32),
        ),
        in_specs=[smem] * 2 + [vmem] * 3,
        out_specs=(vmem, vmem),
        scratch_shapes=[
            pltpu.VMEM((H * KF, 128), F32),
            pltpu.VMEM((H * KF, 128), F32),
            pltpu.VMEM((WIN * KF, 128), F32),
            pltpu.VMEM((WIN, 128, KF), BF16),
            pltpu.VMEM((rows, 128 * nnbr, 128), BF16),
            pltpu.VMEM((rows * 16, 128), F32),
            pltpu.VMEM((rows * 16, 128), F32),
        ],
        compiler_params=params,
        name="smoothing",
    )(
        nbrs.reshape(-1), start - FRONT, whole, ext[:, off : off + rows],
        ext[:, off - REACH : off - REACH + rows - H + WIN],
    )
    totals4 = axis_total(jnp.concatenate([stats, more]), "cells")
    spread, count, cross, energy = [jnp.sum(totals4[i]) for i in range(4)]
    sigma_new = (spread - 2.0 * cross + energy) / (3.0 * count)
    return (motion.reshape(3, nblk * 128), jnp.reshape(sigma_new, (1,)))


def solution(mesh):
    return jax.shard_map(
        body,
        mesh=mesh,
        in_specs=(
            P(None, ("groups", "cells")),
            P(None, ("groups", "cells")),
            P(("groups", "cells"), None),
            P(("groups", "cells")),
            P(("groups", "cells"), None),
            P("groups"),
        ),
        out_specs=(P(None, ("groups", "cells")), P("groups")),
        check_vma=False,
    )
```
